512 devices in a mesh: row: 16 (over z_hi, y), col: 32 (over x, z_lo, core).
Axes of the slice: x: 4, y: 8, z: 8 (z_hi: 2, z_lo: 4; z = z_hi * 4 + z_lo), core: 2. Of those that a mesh axis runs over, the one named last changes fastest.
Arguments:
- inputs: bfloat16 [512, 14848], P('col', 'row'), may hold values from -6 to 6
- weight: bfloat16 [14848, 29696], P('row', 'col'), may hold values from -0.046875 to 0.046875
- cotangent: bfloat16 [512, 29696], P('row', 'col'), may hold values from -6 to 6
Outputs:
- output: bfloat16 [512, 29696], P('row', 'col')
- input_grad: bfloat16 [512, 14848], P('col', 'row')
- weight_grad: bfloat16 [14848, 29696], P('row', 'col')
The draws below stay inside these ranges and needn't reach their ends.
All inputs are finite; a program needn't handle non-finite values.
Results may differ from the reference program's by a relative error of at most 0.001.
Values may be sent and summed in bfloat16 or wider, within the bound.
A program may use at most 64 MiB of HBM per device.

```python
import jax
import jax.numpy as jnp

D = 14848
FF = 29696
TOKENS = 512


def level_of(key, extent, split, least, high):
    loudness, own = 1.0, jax.random.fold_in(key, 6)
    for axis_at, shards_of in split:
        draws = jnp.exp(jax.random.uniform(jax.random.fold_in(own, axis_at), (shards_of,), jnp.float32, least / len(split), high / len(split)))
        loudness = loudness * jnp.repeat(draws, extent[axis_at] // shards_of).reshape([-1 if axis == axis_at else 1 for axis in range(len(extent))])
    return loudness


def normal_values(rng, dims, deviation, bound, pieces=(), dtype=jnp.bfloat16):
    array = deviation * jax.random.normal(rng, dims, jnp.float32)
    if pieces:
        array = array * level_of(rng, dims, pieces, -0.22, 0.18)
    return jnp.clip(array, -bound, bound).astype(dtype)


def setup_inputs(seed: int = 0) -> dict:
    seeds = jax.random.split(jax.random.key(seed), 4)
    inputs = normal_values(seeds[0], (TOKENS, D), 1.0, 6.0, ((0, 32), (1, 16)))
    weight = normal_values(seeds[1], (D, FF), D ** -0.5, 0.046875, ((0, 16), (1, 32)))
    cotangent = normal_values(seeds[2], (TOKENS, FF), 1.0, 6.0, ((0, 16), (1, 32)))
    return {"inputs": inputs, "weight": weight, "cotangent": cotangent}


def reference(inputs, weight, cotangent):
    output = jnp.dot(inputs, weight, preferred_element_type=jnp.float32).astype(jnp.bfloat16)
    input_grad = jnp.dot(cotangent, weight.T, preferred_element_type=jnp.float32).astype(jnp.bfloat16)
    weight_grad = jnp.dot(inputs.T, cotangent, preferred_element_type=jnp.float32).astype(jnp.bfloat16)
    return output, input_grad, weight_grad
```

```python
import jax
import jax.numpy as jnp
from jax import lax
from jax.experimental import pallas as pl
from jax.experimental.pallas import tpu as pltpu
from jax.sharding import PartitionSpec as P

MESH = pl.DeviceIdType.MESH
BF, F32 = jnp.bfloat16, jnp.float32
W = 928
LANES = 1024
SPAN = 173.0
TILES = ((0, 256), (256, 512), (512, 768), (768, 928))


def encode(ref, v):
    a = jnp.abs(v)
    top = jnp.maximum(jnp.max(a, axis=1, keepdims=True) * 1.01, 1e-30).astype(BF).astype(F32)
    code = jnp.exp(a * (SPAN / top) - SPAN / 2)
    ref[:, :W] = jnp.where(v < 0, -code, code).astype(BF)
    ref[:, W:] = jnp.broadcast_to(top, (v.shape[0], LANES - W)).astype(BF)


def decode(coded):
    top = coded[:, W:W + 1].astype(F32)
    code = coded[:, :W].astype(F32)
    a = (jnp.log(jnp.abs(code)) + SPAN / 2) * (top / SPAN)
    return jnp.where(code < 0, -a, a)


def kernel(x_hbm, w_hbm, c_hbm, out_hbm, ig_hbm, wg_hbm,
           G, C, WV, P1, P2, WG, RB, SB, ZB, SR, X1, X2, ZL, OB, IB, ssem, rsem, lsem):
    row, col = lax.axis_index("row"), lax.axis_index("col")
    zh, y = row // 8, row % 8
    x, zl, core = col // 8, (col // 2) % 4, col % 2
    yp, ym = (y + 1) % 8, (y + 7) % 8
    xp, xm, xf = (x + 1) % 4, (x + 3) % 4, (x + 2) % 4
    zp = 1 - zh

    def at(zh_=zh, y_=y, x_=x, zl_=zl, core_=core):
        return (zh_ * 8 + y_, (x_ * 4 + zl_) * 2 + core_)

    right, left, far = at(y_=yp), at(y_=ym), at(zh_=zp)
    xright, xleft, sib = at(x_=xp), at(x_=xm), at(core_=1 - core)
    zpeer = [None] + [at(zl_=(zl + k) % 4) for k in (1, 2, 3)]
    ids, sent = {}, []

    def copy(name, src, dst, dev):
        n = ids.setdefault(name, len(ids))
        return pltpu.make_async_remote_copy(
            src_ref=src, dst_ref=dst, send_sem=ssem.at[n], recv_sem=rsem.at[n],
            device_id=dev, device_id_type=MESH)

    def send(name, src, dst, dev):
        c = copy(name, src, dst, dev)
        c.start()
        sent.append(c)

    def recv(name, dst):
        copy(name, dst, dst, sib).wait_recv()

    own_g = G.at[x * 4 + zl, core]
    own_c = C.at[zh, y]
    load_c = pltpu.make_async_copy(c_hbm, own_c, lsem.at[0])
    load_g = pltpu.make_async_copy(x_hbm, own_g, lsem.at[1])
    load_w = pltpu.make_async_copy(w_hbm, WV, lsem.at[2])
    load_c.start()
    load_g.start()
    barrier = pltpu.get_barrier_semaphore()
    peers = [right, left, far, xright, xleft, sib] + zpeer[1:]
    for dev in peers:
        pl.semaphore_signal(barrier, inc=1, device_id=dev, device_id_type=MESH)
    load_w.start()
    load_c.wait()
    load_g.wait()
    pl.semaphore_wait(barrier, len(peers))

    def gx(xx, lo, n, cc=core):
        return G.at[pl.ds(xx * 4 + lo, n), cc]

    def send_g(name, xx, lo, n, dev):
        send(name, gx(xx, lo, n), gx(xx, lo, n), dev)

    def cs(sub, yy):
        return C.at[zh if sub == 0 else zp, yy % 8]

    def ring_send(sub, sign, s):
        ref = cs(sub, y + 8 - sign * s)
        send(("k", sub, sign, s), ref, ref, right if sign > 0 else left)

    def ring_recv(sub, sign, s):
        recv(("k", sub, sign, s), cs(sub, y + 8 - sign * (s + 1)))

    ring_send(0, 1, 0)
    ring_send(0, -1, 0)
    for k in (1, 2, 3):
        send(("iz", k), own_g, own_g, zpeer[k])
    send("kz", own_c, own_c, far)

    for k in (1, 2, 3):
        recv(("iz", k), G.at[x * 4 + (zl + 4 - k) % 4, core])
    send_g("xp0", x, 0, 4, xright)
    send_g("xm0", x, 0, 4, xleft)
    send_g("s0", x, 0, 4, sib)
    for sign in (1, -1):
        ring_recv(0, sign, 0)
        ring_send(0, sign, 1)
    recv("kz", C.at[zp, y])
    for sign in (1, -1):
        ring_send(1, sign, 0)
    recv("xp0", gx(xm, 0, 4))
    send_g("xp1", xm, 0, 2, xright)
    send_g("s1", xm, 0, 4, sib)
    recv("xm0", gx(xp, 0, 4))
    send_g("xm1", xp, 2, 2, xleft)
    send_g("s2", xp, 0, 4, sib)
    for sign in (1, -1):
        ring_recv(0, sign, 1)
        ring_send(0, sign, 2)
    for sign in (1, -1):
        ring_recv(1, sign, 0)
        ring_send(1, sign, 1)
    recv("xp1", gx(xf, 0, 2))
    send_g("s3", xf, 0, 2, sib)
    recv("xm1", gx(xf, 2, 2))
    send_g("s4", xf, 2, 2, sib)
    load_w.wait()
    other = 1 - core
    recv("s0", gx(x, 0, 4, other))
    recv("s1", gx(xm, 0, 4, other))
    recv("s2", gx(xp, 0, 4, other))
    ring_recv(0, 1, 2)
    ring_send(0, 1, 3)
    recv("s3", gx(xf, 0, 2, other))
    recv("s4", gx(xf, 2, 2, other))

    g = G[...].reshape(512, W)
    for lo, hi in TILES:
        P1[:, lo:hi] = jnp.dot(g, WV[:, lo:hi], preferred_element_type=F32)

    def part(sub, yy):
        first = ((zh if sub == 0 else zp) * 8 + yy % 8) * 32
        return P1[pl.ds(pl.multiple_of(first, 32), 32), :]

    def first_step(sub, sign):
        return 0 if (sub == 1) == (sign > 0) else 1

    def red(sub, sign, s):
        d = 0 if sign > 0 else 1
        v = part(sub, y + 8 + sign * (4 - s))
        if s > first_step(sub, sign):
            recv(("r", sub, sign, s - 1), RB.at[d, sub, s - 1])
            v = v + decode(RB[d, sub, s - 1])
        encode(SB.at[d, sub, s], v)
        send(("r", sub, sign, s), SB.at[d, sub, s], RB.at[d, sub, s], right if sign > 0 else left)

    red(1, 1, 0)
    red(0, -1, 0)
    red(1, -1, 1)
    red(0, 1, 1)
    for sign in (1, -1):
        ring_recv(1, sign, 1)
        ring_send(1, sign, 2)
    red(1, 1, 1)
    ring_recv(0, -1, 2)
    ring_recv(0, 1, 3)
    ring_recv(1, -1, 2)
    ring_send(1, -1, 3)
    red(0, -1, 1)
    red(1, 1, 2)
    red(1, -1, 2)
    ring_recv(1, 1, 2)
    ring_recv(1, -1, 3)

    c = C[...].reshape(512, W)
    for lo, hi in TILES:
        P2[:, :, :, lo:hi] = lax.dot_general(
            c, WV[lo:hi, :], (((1,), (1,)), ((), ())), preferred_element_type=F32
        ).reshape(16, 2, 16, hi - lo)
    order = (xf, xp, xm, x)
    for j, xx in enumerate(order):
        send(("s", j), P2.at[pl.ds(xx * 4, 4), other], SR.at[j], sib)
    red(0, -1, 2)
    red(0, 1, 2)
    red(1, 1, 3)
    red(1, -1, 3)

    def q(j, lo, n):
        v = P2[pl.ds(order[j] * 4 + lo, n), core] + SR[j, lo:lo + n]
        return v.reshape(n * 16, W)

    def xsend(name, slot, v, dev):
        encode(X1.at[slot], v)
        send(name, X1.at[slot], X2.at[slot], dev)

    recv(("s", 0), SR.at[0])
    xsend("x0", 0, q(0, 0, 2), xright)
    xsend("x1", 1, q(0, 2, 2), xleft)
    recv(("s", 1), SR.at[1])
    xsend("x2", 2, q(1, 2, 2), xright)
    recv(("s", 2), SR.at[2])
    xsend("x3", 3, q(2, 0, 2), xleft)
    red(0, -1, 3)
    red(0, 1, 3)
    recv("x0", X2.at[0])
    xsend("x4", 4, q(1, 0, 2) + decode(X2[0]), xright)
    recv("x1", X2.at[1])
    xsend("x5", 5, q(2, 2, 2) + decode(X2[1]), xleft)

    recv(("r", 1, 1, 3), RB.at[0, 1, 3])
    recv(("r", 1, -1, 3), RB.at[1, 1, 3])
    encode(ZB.at[0], part(1, y) + decode(RB[0, 1, 3]) + decode(RB[1, 1, 3]))
    send("rz", ZB.at[0], ZB.at[1], far)

    gg = G[...].reshape(512, W)
    cc = C[...].reshape(512, W)
    for lo, hi in TILES:
        WG[lo:hi, :] = lax.dot_general(
            gg[:, lo:hi], cc, (((0,), (0,)), ((), ())), preferred_element_type=F32
        ).astype(BF)
    store_wg = pltpu.make_async_copy(WG, wg_hbm, lsem.at[3])
    store_wg.start()

    recv(("s", 3), SR.at[3])
    recv("x2", X2.at[2])
    recv("x3", X2.at[3])
    hi_half = q(3, 2, 2) + decode(X2[2])
    lo_half = q(3, 0, 2) + decode(X2[3])
    recv("x4", X2.at[4])
    recv("x5", X2.at[5])
    P2[pl.ds(x * 4, 2), core] = (lo_half + decode(X2[4])).reshape(2, 16, W)
    P2[pl.ds(x * 4 + 2, 2), core] = (hi_half + decode(X2[5])).reshape(2, 16, W)
    for k in (1, 2, 3):
        encode(ZL.at[0, k - 1], P2[x * 4 + (zl + k) % 4, core])
        send(("z", k), ZL.at[0, k - 1], ZL.at[1, k - 1], zpeer[k])

    recv(("r", 0, 1, 3), RB.at[0, 0, 3])
    recv(("r", 0, -1, 3), RB.at[1, 0, 3])
    o = part(0, y) + decode(RB[0, 0, 3]) + decode(RB[1, 0, 3])
    recv("rz", ZB.at[1])
    OB[...] = (o + decode(ZB[1])).astype(BF)
    store_o = pltpu.make_async_copy(OB, out_hbm, lsem.at[4])
    store_o.start()

    v = P2[x * 4 + zl, core]
    for k in (1, 2, 3):
        recv(("z", k), ZL.at[1, k - 1])
        v = v + decode(ZL[1, k - 1])
    IB[...] = v.astype(BF)
    store_i = pltpu.make_async_copy(IB, ig_hbm, lsem.at[5])
    store_i.start()
    for s in sent:
        s.wait_send()
    store_wg.wait()
    store_o.wait()
    store_i.wait()
    assert len(ids) <= ssem.shape[0]


def body(inputs, weight, cotangent):
    any_ = pl.BlockSpec(memory_space=pl.ANY)
    return tuple(pl.pallas_call(
        kernel,
        out_shape=(
            jax.ShapeDtypeStruct((32, W), BF),
            jax.ShapeDtypeStruct((16, W), BF),
            jax.ShapeDtypeStruct((W, W), BF),
        ),
        in_specs=[any_] * 3,
        out_specs=(any_,) * 3,
        scratch_shapes=[
            pltpu.VMEM((16, 2, 16, W), BF),
            pltpu.VMEM((2, 8, 32, W), BF),
            pltpu.VMEM((W, W), BF),
            pltpu.VMEM((512, W), F32),
            pltpu.VMEM((16, 2, 16, W), F32),
            pltpu.VMEM((W, W), BF),
            pltpu.VMEM((2, 2, 4, 32, LANES), BF),
            pltpu.VMEM((2, 2, 4, 32, LANES), BF),
            pltpu.VMEM((2, 32, LANES), BF),
            pltpu.VMEM((4, 4, 16, W), F32),
            pltpu.VMEM((6, 32, LANES), BF),
            pltpu.VMEM((6, 32, LANES), BF),
            pltpu.VMEM((2, 3, 16, LANES), BF),
            pltpu.VMEM((32, W), BF),
            pltpu.VMEM((16, W), BF),
            pltpu.SemaphoreType.DMA((64,)),
            pltpu.SemaphoreType.DMA((64,)),
            pltpu.SemaphoreType.DMA((6,)),
        ],
        compiler_params=pltpu.CompilerParams(
            collective_id=0, has_side_effects=True, vmem_limit_bytes=40 * 2**20),
        cost_estimate=pl.CostEstimate(flops=2650000000, bytes_accessed=4000000, transcendentals=0),
    )(inputs, weight, cotangent))


def solution(mesh):
    placed = (P("col", "row"), P("row", "col"), P("row", "col"))
    return jax.shard_map(
        body,
        mesh=mesh,
        in_specs=placed,
        out_specs=(P("row", "col"), P("col", "row"), P("row", "col")),
        check_vma=False,
    )
```

```python
import jax
import jax.numpy as jnp
from jax import lax
from jax.experimental import pallas as pl
from jax.experimental.pallas import tpu as pltpu
from jax.sharding import PartitionSpec as P

MESH = pl.DeviceIdType.MESH
BF, F32 = jnp.bfloat16, jnp.float32
W = 928
LANES = 1024
SPAN = 173.0
TILES = ((0, 256), (256, 512), (512, 768), (768, 928))
ORDER = ("K0", "I0", "KF", "IZ.2", "IZ.1", "IZ.3", "K.0", "GS", "SW", "KZ", "K.1", "GX.1", "GX.3", "GX.2", "KA.1", "KA.2", "K.2", "GR", "M1", "Q0", "F", "Q1", "KB.1", "KB.2", "K.3", "Q2", "R.1", "KR", "M2", "X.2", "X.1", "X.3", "X.0", "R.2", "Q3", "Y.2", "Y.1", "Y.3", "R.3", "W.0", "W.1", "Y.0", "IG", "W.2", "W.3", "OUT",)


def encode(ref, v):
    a = jnp.abs(v)
    top = jnp.maximum(jnp.max(a, axis=1, keepdims=True) * 1.01, 1e-30).astype(BF).astype(F32)
    code = jnp.exp(a * (SPAN / top) - SPAN / 2)
    ref[:, :W] = jnp.where(v < 0, -code, code).astype(BF)
    ref[:, W:] = jnp.broadcast_to(top, (v.shape[0], LANES - W)).astype(BF)


def decode(coded):
    top = coded[:, W:W + 1].astype(F32)
    code = coded[:, :W].astype(F32)
    a = (jnp.log(jnp.abs(code)) + SPAN / 2) * (top / SPAN)
    return jnp.where(code < 0, -a, a)


def kernel(x_hbm, w_hbm, c_hbm, out_ref, ig_ref, wg_ref,
           G, C, C2, WV, WS, P1, P2, RB, SB, ZB, X1, X2, ZL, ssem, rsem, lsem):
    row, col = lax.axis_index("row"), lax.axis_index("col")
    zh, y = row // 8, row % 8
    x, zl, core = col // 8, (col // 2) % 4, col % 2
    zp, other = 1 - zh, 1 - core
    xs = {1: (x + 1) % 4, 2: (x + 2) % 4, 3: (x + 3) % 4}

    def at(zh_=zh, y_=y, x_=x, zl_=zl, core_=core):
        return (zh_ * 8 + y_, (x_ * 4 + zl_) * 2 + core_)

    ydev = {n: at(y_=(y + 8 + n) % 8) for n in (1, -1, 2, -2)}
    xdev = {k: at(x_=xs[k]) for k in xs}
    zdev = {k: at(zl_=(zl + k) % 4) for k in (1, 2, 3)}
    far, sib = at(zh_=zp), at(core_=other)
    ids, sent = {}, []

    def copy(name, src, dst, dev):
        n = ids.setdefault(name, len(ids))
        return pltpu.make_async_remote_copy(
            src_ref=src, dst_ref=dst, send_sem=ssem.at[n], recv_sem=rsem.at[n],
            device_id=dev, device_id_type=MESH)

    def send(name, src, dst, dev):
        c = copy(name, src, dst, dev)
        c.start()
        sent.append(c)

    def recv(name, dst):
        copy(name, dst, dst, sib).wait_recv()

    def g_at(k, j):
        return G.at[x * 4 + (zl + 4 - k) % 4 if j == 0 else xs[j] * 4 + (zl + 4 - k) % 4, core]

    def g_forward(k):
        for j in (1, 3, 2):
            send(("gx", k, j), g_at(k, 0), g_at(k, 0), xdev[j])

    def z_arrival(k):
        recv(("iz", k), g_at(k, 0))
        g_forward(k)

    def g_row(j, cc):
        return G.at[pl.ds((x if j == 0 else xs[j]) * 4, 4), cc]

    def g_sibling(j):
        send(("gs", j), g_row(j, core), g_row(j, core), sib)

    def x_arrival(j):
        for k in range(4):
            recv(("gx", k, 4 - j), g_at(k, j))
        g_sibling(j)

    def g_complete():
        for j in range(4):
            recv(("gs", j), g_row(j, other))

    def c_at(sub, yy):
        return C.at[zh if sub == 0 else zp, yy % 8]

    def c_half(sub, yy, sign):
        return C.at[zh if sub == 0 else zp, yy % 8, 0 if sign > 0 else 1]

    def k_ref(sign, s):
        yy = y + 8 - sign * s
        return c_at(0, yy) if s < 4 else c_half(0, yy, sign)

    def k_send(sign, s):
        ref = k_ref(sign, s) if s < 3 else c_half(0, y + 8 - sign * s, sign)
        send(("k", sign, s), ref, ref, ydev[sign])

    def k_start():
        for sign in (1, -1):
            k_send(sign, 0)

    def k_step(s):
        for sign in (1, -1):
            recv(("k", sign, s), k_ref(sign, s + 1))
            if s < 3:
                k_send(sign, s + 1)
        if s == 3:
            send("ks", C.at[zh, :, other], C2.at[zh], sib)

    def k_sibling(yy):
        send(("ks", yy), c_at(1, y + 8 + yy).at[other], C2.at[zp, (y + 8 + yy) % 8], sib)

    def k_far():
        recv("kz", c_at(1, y))
        for n in (2, 1):
            for sign in (1, -1):
                send(("ka", n, sign), c_at(1, y), c_at(1, y), ydev[n * sign])
        k_sibling(0)

    def k_near(n):
        for sign in (1, -1):
            recv(("ka", n, sign), c_at(1, y + 8 - n * sign))
        if n == 2:
            for sign in (1, -1):
                ref = c_half(1, y + 8 - 2 * sign, sign)
                send(("kb", 2, sign), ref, ref, ydev[2 * sign])
            for sign in (1, -1):
                ref = c_at(1, y + 8 - 2 * sign)
                send(("kb", 1, sign), ref, ref, ydev[sign])
        for sign in (1, -1):
            k_sibling(-n * sign)

    def k_distant(n):
        for sign in (1, -1):
            if n == 1:
                recv(("kb", 1, sign), c_at(1, y + 8 - 3 * sign))
                k_sibling(-3 * sign)
            else:
                recv(("kb", 2, sign), c_half(1, y + 4, sign))
        if n == 2:
            k_sibling(4)

    def w_sibling():
        send("w", w_hbm, WS, sib)

    def m_output():
        load_w.wait()
        g = G[...].reshape(512, W)
        for lo, hi in TILES:
            P1[:, lo:hi] = jnp.dot(g, WV[:, lo:hi], preferred_element_type=F32)

    def part(sub, yy, p=None):
        first = ((zh if sub == 0 else zp) * 8 + yy % 8) * 32 + (16 if p == 1 else 0)
        n = 32 if p is None else 16
        return P1[pl.ds(pl.multiple_of(first, 16), n), :]

    def r_send(*parts):
        for name, n, sign, v, dev in parts:
            encode(SB.at[n, 0 if sign > 0 else 1, pl.ds(0, v.shape[0])], v)
        for name, n, sign, v, dev in parts:
            at_ = (n, 0 if sign > 0 else 1, pl.ds(0, v.shape[0]))
            send((name, sign), SB.at[at_], RB.at[at_], dev)

    def r_recv(name, n, sign, rows=32):
        recv((name, sign), RB.at[n, 0 if sign > 0 else 1, pl.ds(0, rows)])

    def r_value(n, sign, rows=32):
        return decode(RB[n, 0 if sign > 0 else 1, :rows])

    def with_half(v, half, sign):
        zero = jnp.zeros_like(half)
        return v + jnp.concatenate([half, zero] if sign > 0 else [zero, half], axis=0)

    def r_start():
        r_send(*[("r0", 0, sign, part(0, y + 4, 0 if sign > 0 else 1), ydev[sign]) for sign in (1, -1)])

    def r_step(s):
        rows = 16 if s == 1 else 32
        for sign in (1, -1):
            r_recv(f"r{s - 1}", s - 1, sign, rows)
        sums = []
        for sign in (1, -1):
            v, got = part(0, y + 8 + sign * (4 - s)), r_value(s - 1, sign, rows)
            v = with_half(v, got, sign) if s == 1 else v + got
            sums.append((f"r{s}", s, sign, v, ydev[sign]))
        r_send(*sums)

    def q_start():
        r_send(
            *[("q4", 5, sign, part(1, y + 4, 0 if sign > 0 else 1), ydev[2 * sign]) for sign in (1, -1)],
            *[("q3", 4, sign, part(1, y + 8 + 3 * sign), ydev[sign]) for sign in (1, -1)])

    def q_near():
        r_send(*[("q1", 6, sign, part(1, y + 8 + sign), ydev[sign]) for sign in (1, -1)])

    def q_relay():
        for sign in (1, -1):
            r_recv("q3", 4, sign)
            r_recv("q4", 5, sign, 16)
        sums = []
        for sign in (1, -1):
            v = part(1, y + 8 + 2 * sign) + r_value(4, sign)
            sums.append(("q2", 7, sign, with_half(v, r_value(5, sign, 16), sign), ydev[2 * sign]))
        r_send(*sums)

    def q_far():
        for sign in (1, -1):
            r_recv("q1", 6, sign)
            r_recv("q2", 7, sign)
        v = part(1, y)
        for sign in (1, -1):
            v = v + r_value(6, sign) + r_value(7, sign)
        encode(ZB.at[0], v)
        send("rz", ZB.at[0], ZB.at[1], far)

    def finish_output():
        for sign in (1, -1):
            r_recv("r3", 3, sign)
        v = part(0, y) + r_value(3, 1) + r_value(3, -1)
        recv("rz", ZB.at[1])
        out_ref[...] = (v + decode(ZB[1])).astype(BF)

    def k_complete():
        recv("ks", C2.at[zh])
        for yy in range(-3, 5):
            recv(("ks", yy), C2.at[zp, (y + 8 + yy) % 8])

    def m_input_grad():
        recv("w", WS)
        c = C[:, :, core].reshape(256, W)
        c2 = C2[...].reshape(256, W)
        dims = (((1,), (1,)), ((), ()))
        for lo, hi in TILES:
            t = lax.dot_general(c, WV[lo:hi, :], dims, preferred_element_type=F32)
            t += lax.dot_general(c2, WS[lo:hi, :], dims, preferred_element_type=F32)
            P2[:, :, lo:hi] = t.reshape(16, 16, hi - lo)

    def x_send(dz):
        zd = (zl + dz) % 4
        for j in (1, 3, 2):
            encode(X1.at[dz, j - 1], P2[xs[j] * 4 + zd])
        for j in (1, 3, 2):
            send(("x", dz, j), X1.at[dz, j - 1], X2.at[dz, j - 1], xdev[j])

    def x_sum(dz):
        for j in (1, 3, 2):
            recv(("x", dz, j), X2.at[dz, j - 1])
        v = P2[x * 4 + (zl + dz) % 4]
        for j in (1, 3, 2):
            v = v + decode(X2[dz, j - 1])
        if dz == 0:
            P2[x * 4 + zl] = v
        else:
            encode(ZL.at[0, dz - 1], v)
            send(("z", dz), ZL.at[0, dz - 1], ZL.at[1, dz - 1], zdev[dz])

    def finish_input_grad():
        v = P2[x * 4 + zl]
        for k in (1, 2, 3):
            recv(("z", k), ZL.at[1, k - 1])
            v = v + decode(ZL[1, k - 1])
        ig_ref[...] = v.astype(BF)

    def m_weight_grad(n):
        lo, hi = TILES[n]
        g = G[:, :, :, lo:hi].reshape(512, hi - lo)
        c = C[...].reshape(512, W)
        wg_ref[lo:hi, :] = lax.dot_general(
            g, c, (((0,), (0,)), ((), ())), preferred_element_type=F32).astype(BF)

    own_g = g_at(0, 0)
    loads = [pltpu.make_async_copy(c_hbm.at[pl.ds(16 * p, 16)], C.at[zh, y, p], lsem.at[p]) for p in (0, 1)]
    loads.append(pltpu.make_async_copy(x_hbm, own_g, lsem.at[6]))
    load_w = pltpu.make_async_copy(w_hbm, WV, lsem.at[2])
    for load in loads:
        load.start()
    barrier = pltpu.get_barrier_semaphore()
    peers = list(ydev.values()) + list(xdev.values()) + list(zdev.values()) + [far, sib]
    for dev in peers:
        pl.semaphore_signal(barrier, inc=1, device_id=dev, device_id_type=MESH)
    load_w.start()
    for load in loads:
        load.wait()
    pl.semaphore_wait(barrier, len(peers))

    def start_inputs():
        for k in (2, 1, 3):
            send(("iz", k), own_g, own_g, zdev[k])
        g_forward(0)

    def start_cotangent():
        k_start()

    def start_far():
        send("kz", c_at(0, y), c_at(0, y), far)

    run = {
        "I0": start_inputs, "K0": start_cotangent, "KF": start_far,
        "IZ": z_arrival, "GS": lambda: g_sibling(0), "GX": x_arrival, "GR": g_complete,
        "K": k_step, "KZ": k_far, "KA": k_near, "KB": k_distant, "KR": k_complete, "SW": w_sibling,
        "M1": m_output, "F": r_start, "R": r_step, "Q0": q_start, "Q1": q_near, "Q2": q_relay, "Q3": q_far,
        "OUT": finish_output, "M2": m_input_grad, "X": x_send, "Y": x_sum, "IG": finish_input_grad,
        "W": m_weight_grad,
    }
    for token in ORDER:
        name, *numbers = token.split(".")
        run[name](*map(int, numbers))
    if "M1" not in ORDER:
        load_w.wait()
    for s in sent:
        s.wait_send()
    assert len(ids) <= ssem.shape[0]


def body(inputs, weight, cotangent):
    any_ = pl.BlockSpec(memory_space=pl.ANY)
    hbm = pl.BlockSpec(memory_space=pltpu.HBM)
    results = pl.pallas_call(
        kernel,
        out_shape=tuple(pltpu.VMEM(shape, BF) for shape in ((32, W), (16, W), (W, W))),
        in_specs=[hbm] * 3,
        out_specs=(pl.BlockSpec(memory_space=pltpu.VMEM),) * 3,
        scratch_shapes=[
            pltpu.VMEM((16, 2, 16, W), BF),
            pltpu.VMEM((2, 8, 2, 16, W), BF),
            pltpu.VMEM((2, 8, 16, W), BF),
            pltpu.VMEM((W, W), BF),
            pltpu.VMEM((W, W), BF),
            pltpu.VMEM((512, W), F32),
            pltpu.VMEM((16, 16, W), F32),
            pltpu.VMEM((8, 2, 32, LANES), BF),
            pltpu.VMEM((8, 2, 32, LANES), BF),
            pltpu.VMEM((2, 32, LANES), BF),
            pltpu.VMEM((4, 3, 16, LANES), BF),
            pltpu.VMEM((4, 3, 16, LANES), BF),
            pltpu.VMEM((2, 3, 16, LANES), BF),
            pltpu.SemaphoreType.DMA((112,)),
            pltpu.SemaphoreType.DMA((112,)),
            pltpu.SemaphoreType.DMA((8,)),
        ],
        compiler_params=pltpu.CompilerParams(
            collective_id=0, has_side_effects=True, vmem_limit_bytes=60 * 2**20),
        cost_estimate=pl.CostEstimate(flops=2650000000, bytes_accessed=4000000, transcendentals=0),
    )(inputs, weight, cotangent)
    return tuple(results)


def solution(mesh):
    placed = (P("col", "row"), P("row", "col"), P("row", "col"))
    return jax.shard_map(
        body,
        mesh=mesh,
        in_specs=placed,
        out_specs=(P("row", "col"), P("col", "row"), P("row", "col")),
        check_vma=False,
    )
```

```python
import jax
import jax.numpy as jnp
from jax import lax
from jax.experimental import pallas as pl
from jax.experimental.pallas import tpu as pltpu
from jax.sharding import PartitionSpec as P

MESH = pl.DeviceIdType.MESH
BF, F32 = jnp.bfloat16, jnp.float32
W = 928
LANES = 1024
SPAN = 173.0
TILES = ((0, 256), (256, 512), (512, 768), (768, 928))
ORDER = (
    "K0", "I0", "KF", "IZ.2", "IZ.1", "IZ.3", "K.0", "GS", "SW", "KZ", "K.1", "GX.1", "GX.3", "GX.2", "KA.1", "KA.2", "K.2", "GR", "M1", "Q0", "F", "Q1", "KB.1", "KB.2", "K.3", "Q2", "R.1", "KR", "M2", "X.2", "X.1", "X.3", "X.0", "R.2", "Q3", "Y.2", "Y.1", "Y.3", "R.3", "W.0", "W.1", "Y.0", "W.2", "W.3", "IG", "OUT",
)


def encode(ref, v):
    a = jnp.abs(v)
    top = jnp.maximum(jnp.max(a, axis=1, keepdims=True) * 1.01, 1e-30).astype(BF).astype(F32)
    code = jnp.exp(a * (SPAN / top) - SPAN / 2)
    ref[:, :W] = jnp.where(v < 0, -code, code).astype(BF)
    ref[:, W:] = jnp.broadcast_to(top, (v.shape[0], LANES - W)).astype(BF)


def decode(coded):
    top = coded[:, W:W + 1].astype(F32)
    code = coded[:, :W].astype(F32)
    a = (jnp.log(jnp.abs(code)) + SPAN / 2) * (top / SPAN)
    return jnp.where(code < 0, -a, a)


def kernel(x_hbm, w_hbm, c_hbm, out_ref, ig_ref, wg_ref,
           G, C, C2, WV, WS, P1, P2, RB, SB, ZB, X1, X2, ZL, ssem, rsem, lsem):
    row, col = lax.axis_index("row"), lax.axis_index("col")
    zh, y = row // 8, row % 8
    x, zl, core = col // 8, (col // 2) % 4, col % 2
    zp, other = 1 - zh, 1 - core
    xs = {1: (x + 1) % 4, 2: (x + 2) % 4, 3: (x + 3) % 4}

    def at(zh_=zh, y_=y, x_=x, zl_=zl, core_=core):
        return (zh_ * 8 + y_, (x_ * 4 + zl_) * 2 + core_)

    ydev = {n: at(y_=(y + 8 + n) % 8) for n in (1, -1, 2, -2)}
    xdev = {k: at(x_=xs[k]) for k in xs}
    zdev = {k: at(zl_=(zl + k) % 4) for k in (1, 2, 3)}
    far, sib = at(zh_=zp), at(core_=other)
    ids, sent = {}, []

    def copy(name, src, dst, dev):
        n = ids.setdefault(name, len(ids))
        return pltpu.make_async_remote_copy(
            src_ref=src, dst_ref=dst, send_sem=ssem.at[n], recv_sem=rsem.at[n],
            device_id=dev, device_id_type=MESH)

    def send(name, src, dst, dev):
        c = copy(name, src, dst, dev)
        c.start()
        sent.append(c)

    def recv(name, dst):
        copy(name, dst, dst, sib).wait_recv()

    def g_at(k, j):
        return G.at[x * 4 + (zl + 4 - k) % 4 if j == 0 else xs[j] * 4 + (zl + 4 - k) % 4, core]

    def g_forward(k):
        for j in (1, 3, 2):
            send(("gx", k, j), g_at(k, 0), g_at(k, 0), xdev[j])

    def z_arrival(k):
        recv(("iz", k), g_at(k, 0))
        g_forward(k)

    def g_row(j, cc):
        return G.at[pl.ds((x if j == 0 else xs[j]) * 4, 4), cc]

    def g_sibling(j):
        send(("gs", j), g_row(j, core), g_row(j, core), sib)

    def x_arrival(j):
        for k in range(4):
            recv(("gx", k, 4 - j), g_at(k, j))
        g_sibling(j)

    def g_complete():
        for j in range(4):
            recv(("gs", j), g_row(j, other))

    def c_at(sub, yy):
        return C.at[zh if sub == 0 else zp, yy % 8]

    def c_half(sub, yy, sign):
        return C.at[zh if sub == 0 else zp, yy % 8, 0 if sign > 0 else 1]

    def k_ref(sign, s):
        yy = y + 8 - sign * s
        return c_at(0, yy) if s < 4 else c_half(0, yy, sign)

    def k_send(sign, s):
        ref = k_ref(sign, s) if s < 3 else c_half(0, y + 8 - sign * s, sign)
        send(("k", sign, s), ref, ref, ydev[sign])

    def k_start():
        for sign in (1, -1):
            k_send(sign, 0)

    def k_step(s):
        for sign in (1, -1):
            recv(("k", sign, s), k_ref(sign, s + 1))
            if s < 3:
                k_send(sign, s + 1)
        if s == 3:
            send("ks", C.at[zh, :, other], C2.at[zh], sib)

    def k_sibling(yy):
        send(("ks", yy), c_at(1, y + 8 + yy).at[other], C2.at[zp, (y + 8 + yy) % 8], sib)

    def k_far():
        recv("kz", c_at(1, y))
        for n in (2, 1):
            for sign in (1, -1):
                send(("ka", n, sign), c_at(1, y), c_at(1, y), ydev[n * sign])
        k_sibling(0)

    def k_near(n):
        for sign in (1, -1):
            recv(("ka", n, sign), c_at(1, y + 8 - n * sign))
        if n == 2:
            for sign in (1, -1):
                ref = c_half(1, y + 8 - 2 * sign, sign)
                send(("kb", 2, sign), ref, ref, ydev[2 * sign])
            for sign in (1, -1):
                ref = c_at(1, y + 8 - 2 * sign)
                send(("kb", 1, sign), ref, ref, ydev[sign])
        for sign in (1, -1):
            k_sibling(-n * sign)

    def k_distant(n):
        for sign in (1, -1):
            if n == 1:
                recv(("kb", 1, sign), c_at(1, y + 8 - 3 * sign))
                k_sibling(-3 * sign)
            else:
                recv(("kb", 2, sign), c_half(1, y + 4, sign))
        if n == 2:
            k_sibling(4)

    def w_sibling():
        send("w", w_hbm, WS, sib)

    def m_output():
        load_w.wait()
        g = G[...].reshape(512, W)
        for lo, hi in TILES:
            P1[:, lo:hi] = jnp.dot(g, WV[:, lo:hi], preferred_element_type=F32)

    def part(sub, yy, p=None):
        first = ((zh if sub == 0 else zp) * 8 + yy % 8) * 32 + (16 if p == 1 else 0)
        n = 32 if p is None else 16
        return P1[pl.ds(pl.multiple_of(first, 16), n), :]

    def r_send(*parts):
        for name, n, sign, v, dev in parts:
            encode(SB.at[n, 0 if sign > 0 else 1, pl.ds(0, v.shape[0])], v)
        for name, n, sign, v, dev in parts:
            at_ = (n, 0 if sign > 0 else 1, pl.ds(0, v.shape[0]))
            send((name, sign), SB.at[at_], RB.at[at_], dev)

    def r_recv(name, n, sign, rows=32):
        recv((name, sign), RB.at[n, 0 if sign > 0 else 1, pl.ds(0, rows)])

    def r_value(n, sign, rows=32):
        return decode(RB[n, 0 if sign > 0 else 1, :rows])

    def with_half(v, half, sign):
        zero = jnp.zeros_like(half)
        return v + jnp.concatenate([half, zero] if sign > 0 else [zero, half], axis=0)

    def r_start():
        r_send(*[("r0", 0, sign, part(0, y + 4, 0 if sign > 0 else 1), ydev[sign]) for sign in (1, -1)])

    def r_step(s):
        rows = 16 if s == 1 else 32
        for sign in (1, -1):
            r_recv(f"r{s - 1}", s - 1, sign, rows)
        sums = []
        for sign in (1, -1):
            v, got = part(0, y + 8 + sign * (4 - s)), r_value(s - 1, sign, rows)
            v = with_half(v, got, sign) if s == 1 else v + got
            sums.append((f"r{s}", s, sign, v, ydev[sign]))
        r_send(*sums)

    def q_start():
        r_send(
            *[("q4", 5, sign, part(1, y + 4, 0 if sign > 0 else 1), ydev[2 * sign]) for sign in (1, -1)])
        r_send(
            *[("q3", 4, sign, part(1, y + 8 + 3 * sign), ydev[sign]) for sign in (1, -1)])

    def q_near():
        r_send(*[("q1", 6, sign, part(1, y + 8 + sign), ydev[sign]) for sign in (1, -1)])

    def q_relay():
        for sign in (1, -1):
            r_recv("q3", 4, sign)
            r_recv("q4", 5, sign, 16)
        sums = []
        for sign in (1, -1):
            v = part(1, y + 8 + 2 * sign) + r_value(4, sign)
            sums.append(("q2", 7, sign, with_half(v, r_value(5, sign, 16), sign), ydev[2 * sign]))
        r_send(*sums)

    def q_far():
        for sign in (1, -1):
            r_recv("q1", 6, sign)
            r_recv("q2", 7, sign)
        v = part(1, y)
        for sign in (1, -1):
            v = v + r_value(6, sign) + r_value(7, sign)
        encode(ZB.at[0], v)
        send("rz", ZB.at[0], ZB.at[1], far)

    def finish_output():
        for sign in (1, -1):
            r_recv("r3", 3, sign)
        v = part(0, y) + r_value(3, 1) + r_value(3, -1)
        recv("rz", ZB.at[1])
        out_ref[...] = (v + decode(ZB[1])).astype(BF)

    def k_complete():
        recv("ks", C2.at[zh])
        for yy in range(-3, 5):
            recv(("ks", yy), C2.at[zp, (y + 8 + yy) % 8])

    def m_input_grad():
        recv("w", WS)
        c = C[:, :, core].reshape(256, W)
        c2 = C2[...].reshape(256, W)
        dims = (((1,), (1,)), ((), ()))
        for lo, hi in TILES:
            t = lax.dot_general(c, WV[lo:hi, :], dims, preferred_element_type=F32)
            t += lax.dot_general(c2, WS[lo:hi, :], dims, preferred_element_type=F32)
            P2[:, :, lo:hi] = t.reshape(16, 16, hi - lo)

    def x_send(dz):
        zd = (zl + dz) % 4
        for j in (1, 3, 2):
            encode(X1.at[dz, j - 1], P2[xs[j] * 4 + zd])
        for j in (1, 3, 2):
            send(("x", dz, j), X1.at[dz, j - 1], X2.at[dz, j - 1], xdev[j])

    def x_sum(dz):
        for j in (1, 3, 2):
            recv(("x", dz, j), X2.at[dz, j - 1])
        v = P2[x * 4 + (zl + dz) % 4]
        for j in (1, 3, 2):
            v = v + decode(X2[dz, j - 1])
        if dz == 0:
            P2[x * 4 + zl] = v
        else:
            encode(ZL.at[0, dz - 1], v)
            send(("z", dz), ZL.at[0, dz - 1], ZL.at[1, dz - 1], zdev[dz])

    def finish_input_grad():
        v = P2[x * 4 + zl]
        for k in (1, 2, 3):
            recv(("z", k), ZL.at[1, k - 1])
            v = v + decode(ZL[1, k - 1])
        ig_ref[...] = v.astype(BF)

    def m_weight_grad(n):
        lo, hi = TILES[n]
        g = G[:, :, :, lo:hi].reshape(512, hi - lo)
        c = C[...].reshape(512, W)
        wg_ref[lo:hi, :] = lax.dot_general(
            g, c, (((0,), (0,)), ((), ())), preferred_element_type=F32).astype(BF)

    own_g = g_at(0, 0)
    loads = [pltpu.make_async_copy(c_hbm.at[pl.ds(16 * p, 16)], C.at[zh, y, p], lsem.at[p]) for p in (0, 1)]
    loads.append(pltpu.make_async_copy(x_hbm, own_g, lsem.at[6]))
    load_w = pltpu.make_async_copy(w_hbm, WV, lsem.at[2])
    for load in loads:
        load.start()
    barrier = pltpu.get_barrier_semaphore()
    peers = list(ydev.values()) + list(xdev.values()) + list(zdev.values()) + [far, sib]
    for dev in peers:
        pl.semaphore_signal(barrier, inc=1, device_id=dev, device_id_type=MESH)
    load_w.start()
    for load in loads:
        load.wait()
    pl.semaphore_wait(barrier, len(peers))

    def start_inputs():
        for k in (2, 1, 3):
            send(("iz", k), own_g, own_g, zdev[k])
        g_forward(0)

    def start_cotangent():
        k_start()

    def start_far():
        send("kz", c_at(0, y), c_at(0, y), far)

    run = {
        "I0": start_inputs, "K0": start_cotangent, "KF": start_far,
        "IZ": z_arrival, "GS": lambda: g_sibling(0), "GX": x_arrival, "GR": g_complete,
        "K": k_step, "KZ": k_far, "KA": k_near, "KB": k_distant, "KR": k_complete, "SW": w_sibling,
        "M1": m_output, "F": r_start, "R": r_step, "Q0": q_start, "Q1": q_near, "Q2": q_relay, "Q3": q_far,
        "OUT": finish_output, "M2": m_input_grad, "X": x_send, "Y": x_sum, "IG": finish_input_grad,
        "W": m_weight_grad,
    }
    for token in ORDER:
        name, *numbers = token.split(".")
        run[name](*map(int, numbers))
    if "M1" not in ORDER:
        load_w.wait()
    for s in sent:
        s.wait_send()
    assert len(ids) <= ssem.shape[0]


def body(inputs, weight, cotangent):
    any_ = pl.BlockSpec(memory_space=pl.ANY)
    hbm = pl.BlockSpec(memory_space=pltpu.HBM)
    results = pl.pallas_call(
        kernel,
        out_shape=tuple(pltpu.VMEM(shape, BF) for shape in ((32, W), (16, W), (W, W))),
        in_specs=[hbm] * 3,
        out_specs=(pl.BlockSpec(memory_space=pltpu.VMEM),) * 3,
        scratch_shapes=[
            pltpu.VMEM((16, 2, 16, W), BF),
            pltpu.VMEM((2, 8, 2, 16, W), BF),
            pltpu.VMEM((2, 8, 16, W), BF),
            pltpu.VMEM((W, W), BF),
            pltpu.VMEM((W, W), BF),
            pltpu.VMEM((512, W), F32),
            pltpu.VMEM((16, 16, W), F32),
            pltpu.VMEM((8, 2, 32, LANES), BF),
            pltpu.VMEM((8, 2, 32, LANES), BF),
            pltpu.VMEM((2, 32, LANES), BF),
            pltpu.VMEM((4, 3, 16, LANES), BF),
            pltpu.VMEM((4, 3, 16, LANES), BF),
            pltpu.VMEM((2, 3, 16, LANES), BF),
            pltpu.SemaphoreType.DMA((112,)),
            pltpu.SemaphoreType.DMA((112,)),
            pltpu.SemaphoreType.DMA((8,)),
        ],
        compiler_params=pltpu.CompilerParams(
            collective_id=0, has_side_effects=True, vmem_limit_bytes=60 * 2**20),
        cost_estimate=pl.CostEstimate(flops=2650000000, bytes_accessed=4000000, transcendentals=0),
    )(inputs, weight, cotangent)
    return tuple(results)


def solution(mesh):
    placed = (P("col", "row"), P("row", "col"), P("row", "col"))
    return jax.shard_map(
        body,
        mesh=mesh,
        in_specs=placed,
        out_specs=(P("row", "col"), P("col", "row"), P("row", "col")),
        check_vma=False,
    )
```
